32 devices in a mesh: groups: 2 (over x), section: 8 (over z, y), sub: 2 (over core).
Axes of the slice: x: 2, y: 2, z: 4, core: 2. Of those that a mesh axis runs over, the one named last changes fastest.
Arguments:
- voltages: bfloat16 [2048, 2, 65920], P(('groups', 'section', 'sub')), parts along dimension 0, may hold values from -6 to 6
- prototype: float32 [512], replicated, may hold values from 0.02 to 0.07
- beam_weights: bfloat16 [256, 2, 1024, 1024], P(('groups', 'section', 'sub')), parts along dimension 0, may hold values from -0.125 to 0.125
- input_order: int32 [1024], replicated, may hold values from 0 to 1023, each once
- beam_order: int32 [1024], replicated, may hold values from 0 to 1023, each once
- trial_delays: int32 [256, 128], replicated, may hold values from 0 to 127, as said below
Outputs:
- dedispersed: float32 [256, 2048, 128], P(None, ('groups', 'section', 'sub')), parts along dimension 1
The draws below stay inside these ranges and needn't reach their ends.
There are 2 independent parts, one for each index of `groups`. The reference program is written for one: setup_inputs(seed, part) draws one part's arguments, and reference() takes and returns one part's arrays. A program takes and returns all parts, laid end to end along the dimension named above; an argument that names none is the same for every part. Nothing has to cross between parts.
Inputs may be any that keep to these rules, and one draw needn't show every extreme that they name: `input_order`: each physical input appears once. `beam_order`: each physical beam appears once. `trial_delays`: for each trial the delays do not rise with the channel index.
All inputs are finite; a program needn't handle non-finite values.
Results may differ from the reference program's by a relative error of at most 0.0043.
Values may be sent and summed in bfloat16 or wider, within the bound.
A program may use at most 256 MiB of HBM per device.

```python
import math
import jax
import jax.numpy as jnp
from jax import lax

CHANS = 128
INPUTS = 1024
BEAMS = 1024
TRIALS = 256
TAPS = 4
DOWN = 4
SPECTRA = 512
BINS = 128
RAW_LEN = 65920


def draw_trial_delays(key, part):
    top_key = jax.random.fold_in(key, 7)
    value_key = jax.random.fold_in(key, 11)
    top_values = jax.random.randint(top_key, (TRIALS,), BINS // 4, BINS, dtype=jnp.int32)
    top_values = top_values.at[0].set(BINS - 1)
    raw_values = jax.random.randint(value_key, (TRIALS, CHANS), 0, top_values[:, None] + 1, dtype=jnp.int32)
    ordered = -jnp.sort(-raw_values, axis=1)
    ordered = ordered.at[0, 0].set(BINS - 1)
    ordered = ordered.at[0, CHANS - 1].set(0)
    return ordered


def steps_of(rng, extent, cuts, smallest, largest):
    loudness, own = 1.0, jax.random.fold_in(rng, 6)
    for dim, parts in cuts:
        steps = jnp.exp(jax.random.uniform(jax.random.fold_in(own, dim), (parts,), jnp.float32, smallest / len(cuts), largest / len(cuts)))
        loudness = loudness * jnp.repeat(steps, extent[dim] // parts).reshape([-1 if axis == dim else 1 for axis in range(len(extent))])
    return loudness


def scatter_about(own_key, dims, width, most, split=(), held_as=jnp.bfloat16):
    values = width * jax.random.normal(own_key, dims, jnp.float32)
    if split:
        values = values * steps_of(own_key, dims, split, -0.22, 0.18)
    return jnp.clip(values, -most, most).astype(held_as)


def setup_inputs(seed: int = 0, part: int = 0) -> dict:
    keys = jax.random.split(jax.random.key(seed), 7)
    part_splits = jax.random.split(jax.random.fold_in(keys[6], part), 7)
    return {
        "voltages": scatter_about(part_splits[0], (INPUTS, 2, RAW_LEN), 1.0, 6.0, ((0, 16),)),
        "prototype": jnp.clip(jax.random.uniform(keys[1], (TAPS * CHANS,), jnp.float32, 0.02, 0.07), 0.02, 0.07),
        "beam_weights": scatter_about(part_splits[2], (CHANS, 2, BEAMS, INPUTS), (2 * INPUTS) ** -0.5, 0.125, ((0, 16),)),
        "input_order": jax.random.permutation(keys[3], INPUTS).astype(jnp.int32),
        "beam_order": jax.random.permutation(keys[4], BEAMS).astype(jnp.int32),
        "trial_delays": draw_trial_delays(jax.random.fold_in(keys[6], 71), part),
    }


def filter_matrix(prototype):
    channel_index = jnp.arange(CHANS, dtype=jnp.int32)
    phase_step = channel_index[:, None] * channel_index[None, :] % CHANS
    angles = 2.0 * math.pi / CHANS * phase_step.astype(jnp.float32)
    cosine = jnp.tile(jnp.cos(angles), (1, TAPS)) * prototype[None, :]
    sine_part = jnp.tile(jnp.sin(angles), (1, TAPS)) * prototype[None, :]
    real_rows = jnp.concatenate([cosine, sine_part], axis=1)
    imag_rows = jnp.concatenate([-sine_part, cosine], axis=1)
    return jnp.stack([real_rows, imag_rows], axis=0).astype(jnp.bfloat16)

def channelize(block_volts, matrix):
    input_count = block_volts.shape[0]
    frames = block_volts.reshape(input_count, 2, SPECTRA + TAPS - 1, CHANS)
    windows = jnp.concatenate([frames[:, part_index, tap_index:tap_index + SPECTRA, :] for part_index in range(2) for tap_index in range(TAPS)], axis=2)
    result = lax.dot_general(matrix.astype(jnp.float32), windows.astype(jnp.float32), (((2,), (2,)), ((), ())), preferred_element_type=jnp.float32)
    return result.astype(jnp.bfloat16)

def reference(voltages, prototype, beam_weights, input_order, beam_order, trial_delays):
    matrix = filter_matrix(prototype)
    grouped = voltages.reshape(INPUTS // 8, 8, 2, RAW_LEN)

    def channelize_block(block_volts):
        return channelize(block_volts, matrix)
    pieces = lax.map(channelize_block, grouped)
    channelized = jnp.transpose(pieces, (2, 1, 0, 3, 4)).reshape(CHANS, 2, INPUTS, SPECTRA)

    def one_channel(operands):
        weights_here, volts_here = operands
        picked = jnp.take(jnp.take(weights_here, beam_order, axis=1), input_order, axis=2)
        beam_real = jnp.dot(picked[0], volts_here[0], preferred_element_type=jnp.float32) - jnp.dot(picked[1], volts_here[1], preferred_element_type=jnp.float32)
        beam_imag = jnp.dot(picked[0], volts_here[1], preferred_element_type=jnp.float32) + jnp.dot(picked[1], volts_here[0], preferred_element_type=jnp.float32)
        power = beam_real * beam_real + beam_imag * beam_imag
        return power.reshape(BEAMS, BINS, DOWN).sum(axis=2)
    folded = lax.map(one_channel, (beam_weights, channelized))
    centred = folded - lax.optimization_barrier(jnp.mean(folded, axis=2, keepdims=True))
    spread = lax.optimization_barrier(jnp.mean(centred * centred, axis=2, keepdims=True))
    normed = centred / jnp.sqrt(spread + 1e-06)
    sample_index = jnp.arange(BINS, dtype=jnp.int32)

    def one_trial(delays):
        row_map = (sample_index[None, :] + delays[:, None].astype(jnp.int32)) % BINS
        shifted = jnp.take_along_axis(normed, jnp.broadcast_to(row_map[:, None, :], normed.shape), axis=2)
        return lax.optimization_barrier(jnp.sum(shifted, axis=0)) / math.sqrt(CHANS)
    return lax.map(one_trial, trial_delays)
```

```python
import functools
import math

import jax
import jax.numpy as jnp
import numpy as np
from jax import lax
from jax.experimental import pallas as pl
from jax.experimental.pallas import tpu as pltpu
from jax.sharding import PartitionSpec as P

CHANS = 128
INPUTS = 1024
BEAMS = 1024
TAPS = 4
DOWN = 4
SPECTRA = 512
BINS = 128
SLOTS = 8
MESH = pl.DeviceIdType.MESH
NT = (((1,), (1,)), ((), ()))
NN = (((1,), (0,)), ((), ()))


def filter_matrix(prototype):
    channel_index = np.arange(CHANS)
    phase_step = channel_index[:, None] * channel_index[None, :] % CHANS
    angles = 2.0 * math.pi / CHANS * phase_step
    cosine = np.tile(np.cos(angles), (1, TAPS))
    sine = np.tile(np.sin(angles), (1, TAPS))
    table = np.concatenate(
        [np.concatenate([cosine, sine], axis=1), np.concatenate([-sine, cosine], axis=1)], axis=0
    ).astype(np.float32)
    return (table * jnp.tile(prototype, 2)[None, :]).astype(jnp.bfloat16)


def dot(a, b, dims=NN):
    return lax.dot_general(a, b, dims, preferred_element_type=jnp.float32)


def exchange_kernel(
    owners,
    subs,
    frames_ref,
    filter_ref,
    weights_ref,
    pick_ref,
    beams_ref,
    series_ref,
    landing_ref,
    frame_buf,
    wide,
    stage,
    outbox,
    weight_buf,
    steered,
    spectra,
    normed,
    power,
    frame_sem,
    weight_sem,
    own_sem,
    load_sem,
    early_send_sem,
    early_recv_sem,
    send_sem,
    recv_sem,
    power_own_sem,
    power_send_sem,
    power_recv_sem,
):
    inputs = frames_ref.shape[0]
    chan_dev = weights_ref.shape[0]
    group = min(16, inputs)
    blocks = inputs // group
    me = lax.axis_index("section") * subs + lax.axis_index("sub")

    def place(owner):
        return {"section": owner // subs, "sub": owner % subs}

    def partner(step):
        return (me + step) % owners

    barrier = pltpu.get_barrier_semaphore()

    def greet(step, carry):
        pl.semaphore_signal(
            barrier, inc=1, device_id=place((me + step) % owners), device_id_type=MESH
        )
        return carry

    lax.fori_loop(1, owners, greet, 0)

    def frame_copy(index):
        slot = index % SLOTS
        return pltpu.make_async_copy(
            frames_ref.at[index], frame_buf.at[slot], frame_sem.at[slot]
        )

    def weight_copy(chan):
        slot = chan % 2
        return pltpu.make_async_copy(
            weights_ref.at[chan], weight_buf.at[slot], weight_sem.at[slot]
        )

    def spectra_copy(chan, owner, source):
        return pltpu.make_async_remote_copy(
            src_ref=outbox.at[owner * chan_dev + chan],
            dst_ref=landing_ref.at[chan, source],
            send_sem=send_sem.at[chan, owner],
            recv_sem=recv_sem.at[chan, source],
            device_id=place(owner),
            device_id_type=MESH,
        )

    def early_copy(block, owner, source):
        rows = pl.ds(pl.multiple_of(block * 2 * group, 2 * group), 2 * group)
        return pltpu.make_async_remote_copy(
            src_ref=outbox.at[owner * chan_dev, rows],
            dst_ref=landing_ref.at[0, source, rows],
            send_sem=early_send_sem.at[block, owner],
            recv_sem=early_recv_sem.at[block, source],
            device_id=place(owner),
            device_id_type=MESH,
        )

    def own_copy(chan):
        return pltpu.make_async_copy(
            outbox.at[me * chan_dev + chan], landing_ref.at[chan, me], own_sem.at[chan]
        )

    def power_copy(chan, owner, source):
        return pltpu.make_async_remote_copy(
            src_ref=power.at[chan, owner],
            dst_ref=series_ref.at[source * chan_dev + chan],
            send_sem=power_send_sem.at[chan, owner],
            recv_sem=power_recv_sem.at[chan, source],
            device_id=place(owner),
            device_id_type=MESH,
        )

    def power_own_copy(chan):
        return pltpu.make_async_copy(
            power.at[chan, me], series_ref.at[me * chan_dev + chan], power_own_sem.at[chan]
        )

    for index in range(min(SLOTS - 1, inputs)):
        frame_copy(index).start()
    weight_copy(0).start()

    def channelize(index, slot, member):
        edges = []
        for part in range(2):
            wide[part] = frame_buf[slot, part].astype(jnp.float32)
            edges.append(
                [
                    wide[part, pl.ds(s, BINS, stride=DOWN), :].astype(jnp.bfloat16)
                    for s in range(DOWN + TAPS - 1)
                ]
            )
        for m in range(DOWN):
            window = jnp.concatenate(edges[0][m : m + TAPS] + edges[1][m : m + TAPS], axis=1)
            stage[m, pl.ds(member, 2 * CHANS, stride=group), :] = dot(
                filter_ref[...], window, NT
            )

    def input_group(block, carry):
        def one(member, inner):
            index = block * group + member
            frame_copy(index).wait()

            @pl.when(index + SLOTS - 1 < inputs)
            def _():
                frame_copy(index + SLOTS - 1).start()

            channelize(index, index % SLOTS, member)
            return inner

        lax.fori_loop(0, group, one, 0)

        def spread(chan, inner):
            halves = []
            for p in range(2):
                at_row = pl.ds(pl.multiple_of((p * CHANS + chan) * group, group), group)
                halves.append(
                    jnp.concatenate([stage[m, at_row, :] for m in range(DOWN)], axis=1)
                )
            row = pl.multiple_of(block * 2 * group, 2 * group)
            outbox[chan, pl.ds(row, 2 * group), :] = jnp.concatenate(halves, axis=0).astype(
                jnp.bfloat16
            )
            return inner

        lax.fori_loop(0, CHANS, spread, 0, unroll=4)

        def send_early(step, inner):
            early_copy(block, partner(step), me).start()
            return inner

        lax.fori_loop(1, owners, send_early, 0)
        return carry

    pl.semaphore_wait(barrier, owners - 1)
    lax.fori_loop(0, blocks, input_group, 0)
    own_copy(0).start()

    def send_channel(chan, carry):
        own_copy(chan).start()

        def send(step, inner):
            spectra_copy(chan, partner(step), me).start()
            return inner

        lax.fori_loop(1, owners, send, 0)
        return carry

    lax.fori_loop(1, chan_dev, send_channel, 0)

    columns = 512
    rows = 256
    lane = lax.broadcasted_iota(jnp.int32, (rows, columns), 1)

    def one_channel(chan, carry):
        slot = chan % 2
        weight_copy(chan).wait()

        @pl.when(chan + 1 < chan_dev)
        def _():
            weight_copy(chan + 1).start()

        def steer_rows(tile, inner):
            at_row = pl.ds(pl.multiple_of(tile * rows, rows), rows)
            real = weight_buf[slot, 0, at_row, :]
            imag = weight_buf[slot, 1, at_row, :]
            for start in range(0, 2 * INPUTS, columns):
                pick = pick_ref[:, start : start + columns]
                picked_real = dot(real, pick)
                picked_imag = dot(imag, pick)
                first = ((lane + start) // group) % 2 == 0
                steered[0, at_row, start : start + columns] = jnp.where(
                    first, picked_real, -picked_imag
                ).astype(jnp.bfloat16)
                steered[1, at_row, start : start + columns] = jnp.where(
                    first, picked_imag, picked_real
                ).astype(jnp.bfloat16)
            return inner

        lax.fori_loop(0, BEAMS // rows, steer_rows, 0)

        own_copy(chan).wait()

        def arrive(step, inner):
            source = (me + step) % owners

            @pl.when(chan == 0)
            def _():
                for block in range(blocks):
                    early_copy(block, source, source).wait_recv()

            @pl.when(chan > 0)
            def _():
                spectra_copy(chan, source, source).wait_recv()

            return inner

        lax.fori_loop(1, owners, arrive, 0)
        load = pltpu.make_async_copy(landing_ref.at[chan], spectra, load_sem)
        load.start()
        load.wait()

        def form_rows(tile, inner):
            at_row = pl.ds(pl.multiple_of(tile * rows, rows), rows)
            field = spectra[...].reshape(2 * INPUTS, SPECTRA)
            real = dot(steered[0, at_row, :], field)
            imag = dot(steered[1, at_row, :], field)
            squares = real * real + imag * imag
            folded = squares[:, 0:BINS]
            for m in range(1, DOWN):
                folded = folded + squares[:, m * BINS : (m + 1) * BINS]
            centred = folded - jnp.mean(folded, axis=1, keepdims=True)
            spread = jnp.mean(centred * centred, axis=1, keepdims=True)
            normed[at_row, :] = (centred / jnp.sqrt(spread + 1e-06)).astype(jnp.bfloat16)
            return inner

        lax.fori_loop(0, BEAMS // rows, form_rows, 0)
        stored = dot(beams_ref[...], normed[...])
        power[chan] = stored.reshape(power.shape[1:]).astype(jnp.bfloat16)
        power_own_copy(chan).start()

        def send(step, inner):
            power_copy(chan, partner(step), me).start()
            return inner

        lax.fori_loop(1, owners, send, 0)
        return carry

    lax.fori_loop(0, chan_dev, one_channel, 0)

    def finish(chan, carry):
        power_own_copy(chan).wait()

        def drain(step, inner):
            other = (me + step) % owners

            @pl.when(chan == 0)
            def _():
                for block in range(blocks):
                    early_copy(block, other, me).wait_send()

            @pl.when(chan > 0)
            def _():
                spectra_copy(chan, other, me).wait_send()

            power_copy(chan, other, me).wait_send()
            power_copy(chan, other, other).wait_recv()
            return inner

        lax.fori_loop(1, owners, drain, 0)
        return carry

    lax.fori_loop(0, chan_dev, finish, 0)


def exchange(frames, matrix, beam_weights, pick, beams, owners, subs):
    inputs = frames.shape[0]
    chan_dev = beam_weights.shape[0]
    beam_dev = BEAMS // owners
    group = min(16, inputs)
    any_space = pl.BlockSpec(memory_space=pl.ANY)
    vmem = pl.BlockSpec(memory_space=pltpu.VMEM)
    series, _ = pl.pallas_call(
        functools.partial(exchange_kernel, owners, subs),
        out_shape=(
            jax.ShapeDtypeStruct((CHANS, beam_dev, BINS), jnp.bfloat16),
            jax.ShapeDtypeStruct((chan_dev, owners, 2 * inputs, SPECTRA), jnp.bfloat16),
        ),
        in_specs=[any_space, vmem, any_space, vmem, vmem],
        out_specs=(any_space, any_space),
        scratch_shapes=[
            pltpu.VMEM((SLOTS,) + frames.shape[1:], jnp.bfloat16),
            pltpu.VMEM(frames.shape[1:], jnp.float32),
            pltpu.VMEM((DOWN, 2 * CHANS * group, BINS), jnp.float32),
            pltpu.VMEM((CHANS, 2 * inputs, SPECTRA), jnp.bfloat16),
            pltpu.VMEM((2, 2, BEAMS, INPUTS), jnp.bfloat16),
            pltpu.VMEM((2, BEAMS, 2 * INPUTS), jnp.bfloat16),
            pltpu.VMEM((owners, 2 * inputs, SPECTRA), jnp.bfloat16),
            pltpu.VMEM((BEAMS, BINS), jnp.bfloat16),
            pltpu.VMEM((chan_dev, owners, beam_dev, BINS), jnp.bfloat16),
            pltpu.SemaphoreType.DMA((SLOTS,)),
            pltpu.SemaphoreType.DMA((2,)),
            pltpu.SemaphoreType.DMA((chan_dev,)),
            pltpu.SemaphoreType.DMA,
            pltpu.SemaphoreType.DMA((inputs // group, owners)),
            pltpu.SemaphoreType.DMA((inputs // group, owners)),
            pltpu.SemaphoreType.DMA((chan_dev, owners)),
            pltpu.SemaphoreType.DMA((chan_dev, owners)),
            pltpu.SemaphoreType.DMA((chan_dev,)),
            pltpu.SemaphoreType.DMA((chan_dev, owners)),
            pltpu.SemaphoreType.DMA((chan_dev, owners)),
        ],
        compiler_params=pltpu.CompilerParams(
            collective_id=0, has_side_effects=True, vmem_limit_bytes=60 * 1024 * 1024
        ),
        name="exchange",
    )(frames, matrix, beam_weights, pick, beams)
    return series


def split_pair(array):
    high = array.astype(jnp.bfloat16)
    low = (array - high.astype(np.float64)).astype(jnp.bfloat16)
    return high, low


def dedisperse_kernel(
    series_ref, turn_ref, forward_ref, inverse_ref, out_ref, spectrum, turned, phase
):
    beams = series_ref.shape[1]
    trials = turn_ref.shape[1]
    half = BINS // 2 + 1
    joined = BINS // beams
    chan_rows = CHANS // joined
    trial_rows = trials // joined

    def transform(row, carry):
        block = jnp.concatenate(
            [series_ref[r * chan_rows + row].astype(jnp.float32) for r in range(joined)], axis=0
        ).astype(jnp.bfloat16)
        spectrum[pl.ds(row, BINS, stride=chan_rows), :] = dot(
            forward_ref[0], block, NT
        ) + dot(forward_ref[1], block, NT)
        return carry

    lax.fori_loop(0, chan_rows, transform, 0, unroll=4)

    def slab(index):
        rows = spectrum[pl.ds(pl.multiple_of(index * chan_rows, chan_rows), chan_rows), :]
        return jnp.concatenate(
            [rows[:, r * beams : (r + 1) * beams] for r in range(joined)], axis=0
        ).astype(jnp.bfloat16)

    def put(index, value):
        turned[pl.ds(pl.multiple_of(index * trial_rows, trial_rows), trial_rows), :] = (
            jnp.concatenate(
                [value[r * trial_rows : (r + 1) * trial_rows] for r in range(joined)], axis=1
            )
        )

    ones = jnp.ones((trials, CHANS), jnp.bfloat16)
    put(0, dot(ones, slab(0)))
    phase[...] = turn_ref[...]

    def rotate(freq, carry):
        cos_now = phase[0]
        sin_now = phase[1]
        cos_half = cos_now.astype(jnp.bfloat16)
        sin_half = sin_now.astype(jnp.bfloat16)
        both = jnp.concatenate([slab(freq), slab(freq + half - 1)], axis=0)
        put(freq, dot(jnp.concatenate([cos_half, -sin_half], axis=1), both))
        put(freq + half - 1, dot(jnp.concatenate([sin_half, cos_half], axis=1), both))
        phase[0] = cos_now * turn_ref[0] - sin_now * turn_ref[1]
        phase[1] = cos_now * turn_ref[1] + sin_now * turn_ref[0]
        return carry

    lax.fori_loop(1, half - 1, rotate, 0)
    put(half - 1, dot(phase[0].astype(jnp.bfloat16), slab(half - 1)))

    def restore(row, carry):
        rows = turned[pl.ds(row, BINS, stride=trial_rows), :].astype(jnp.bfloat16)
        rows = jnp.concatenate([rows, rows], axis=0)
        result = dot(rows, inverse_ref[...], (((0,), (0,)), ((), ())))
        for r in range(joined):
            out_ref[r * trial_rows + row] = result[r * beams : (r + 1) * beams]
        return carry

    lax.fori_loop(0, trial_rows, restore, 0, unroll=4)


def dedisperse(series, trial_delays):
    half = BINS // 2 + 1
    beams = series.shape[1]
    trials = trial_delays.shape[0]
    sample_index = np.arange(BINS)
    freq_index = np.arange(half)
    angles = 2.0 * math.pi / BINS * (freq_index[:, None] * sample_index[None, :] % BINS)
    forward = np.concatenate([np.cos(angles), -np.sin(angles)[1 : half - 1]], axis=0)
    edge = (freq_index == 0) | (freq_index == BINS // 2)
    fold_weight = np.where(edge, 1.0, 2.0) / BINS / math.sqrt(CHANS)
    inverse = np.concatenate([fold_weight, fold_weight[1 : half - 1]])[:, None] * forward
    turn_angle = 2.0 * math.pi / BINS * trial_delays.astype(jnp.float32)
    turn = jnp.stack([jnp.cos(turn_angle), jnp.sin(turn_angle)])
    vmem = pl.BlockSpec(memory_space=pltpu.VMEM)
    return pl.pallas_call(
        dedisperse_kernel,
        out_shape=jax.ShapeDtypeStruct((trials, beams, BINS), jnp.float32),
        in_specs=[vmem] * 4,
        out_specs=vmem,
        scratch_shapes=[
            pltpu.VMEM((BINS * CHANS * beams // BINS, BINS), jnp.float32),
            pltpu.VMEM((BINS * trials * beams // BINS, BINS), jnp.float32),
            pltpu.VMEM((2, trials, CHANS), jnp.float32),
        ],
        compiler_params=pltpu.CompilerParams(vmem_limit_bytes=56 * 1024 * 1024),
        name="dedisperse",
    )(
        series,
        turn,
        np.stack(split_pair(forward)),
        np.concatenate(split_pair(inverse), axis=0),
    )


def shards(voltages, prototype, beam_weights, input_order, beam_order, trial_delays):
    subs = lax.axis_size("sub")
    owners = lax.axis_size("section") * subs
    inputs = voltages.shape[0]
    frames = voltages.reshape(inputs, 2, SPECTRA + TAPS - 1, CHANS)
    physical = jnp.arange(INPUTS, dtype=jnp.int32)
    group = min(16, inputs)
    by_block = jnp.broadcast_to(
        input_order.reshape(INPUTS // group, 1, group), (INPUTS // group, 2, group)
    ).reshape(2 * INPUTS)
    pick = (physical[:, None] == by_block[None, :]).astype(jnp.bfloat16)
    beams = (beam_order[:, None] == physical[None, :]).astype(jnp.bfloat16)
    series = exchange(
        frames, filter_matrix(prototype), beam_weights, pick, beams, owners, subs
    )
    return dedisperse(series, trial_delays)


def solution(mesh):
    return jax.shard_map(
        shards,
        mesh=mesh,
        in_specs=(
            P(("groups", "section", "sub"), None, None),
            P(),
            P(("groups", "section", "sub"), None, None, None),
            P(),
            P(),
            P(),
        ),
        out_specs=P(None, ("groups", "section", "sub"), None),
        check_vma=False,
    )
```
